32 devices in a mesh: req: 8 (over z, x), head: 4 (over y, core).
Axes of the slice: x: 2, y: 2, z: 4, core: 2. Of those that a mesh axis runs over, the one named last changes fastest.
Arguments:
- tokens: bfloat16 [8192, 1536], P('req', 'head'), may hold values from -6 to 6
- new_counts: int32 [8, 4], P('req'), may hold values from 1 to 512, 1024 in all within a row
- kv_cache: bfloat16 [32, 8, 7680, 128], P('req', 'head'), may hold values from -300 to 300
- norm_attn: float32 [1536], replicated, may hold values from 0.1 to 1.9
- query_weight: bfloat16 [1536, 8, 192], P(None, 'head'), may hold values from -0.15625 to 0.15625
- key_value_weight: bfloat16 [1536, 8, 128], P(None, 'head'), may hold values from -0.4375 to 0.4375
- output_weight: bfloat16 [8, 192, 1536], P('head'), may hold values from -0.15625 to 0.15625
- norm_moe: float32 [1536], replicated, may hold values from 0.1 to 1.9
- routes: int32 [8192, 8], P(('req', 'head')), may hold values from 0 to 31, all different within a row; in each aligned block of 256 rows (0 to 255, 256 to 511, ...) at most 128 rows name the same one
- route_gain: float32 [8192, 8], P(('req', 'head')), may hold values from 0.03 to 0.3
- w_gate_up: bfloat16 [32, 1536, 1024], P('req'), may hold values from -0.15625 to 0.15625
- w_down: bfloat16 [32, 512, 1536], P('req'), may hold values from -0.25 to 0.25
Outputs:
- mixed: bfloat16 [8192, 1536], P(('req', 'head'))
The draws below stay inside these ranges and needn't reach their ends.
Inputs may be any that keep to these rules, and one draw needn't show every extreme that they name: `new_counts`: the 4 counts of one index of req sum to 1024, and one of them is exactly 512. `routes`: the 8 experts of a row differ. In each aligned block of 256 rows (the rows of one device) no expert is named more than 128 times, a bound that some block reaches.
All inputs are finite; a program needn't handle non-finite values.
Results may differ from the reference program's by a relative error of at most 0.019.
Values may be sent and summed in bfloat16 or wider, within the bound.
A program may use at most 192 MiB of HBM per device.

```python
import math
import jax
import jax.numpy as jnp
import numpy as np
from jax import lax

MODEL_DIM = 1536
QUERY_HEADS = 24
KEY_HEADS = 8
HEAD_DIM = 64
FF = 512
EXPERTS = 32
TOPK = 8
RATIO = 15
REQ_DEV = 4
TOK_DEV = 1024
QUERY_PER_KV = 3
MOSTN = 512
CACHE_SLOTS = 7680
MT = 256
CAP = 128
TOKENS = 8192
REQUEST_TOTAL = 32
N_HEAD = 4


def draw_kv_cache(key, part):
    key_primary = jax.random.fold_in(key, 11)
    value_rows = jnp.clip(jax.random.normal(key_primary, (REQUEST_TOTAL, KEY_HEADS, CACHE_SLOTS, 2 * HEAD_DIM), jnp.float32), -6.0, 6.0)
    key_scaling = jnp.full((REQUEST_TOTAL, KEY_HEADS, CACHE_SLOTS, 1), 2.5, jnp.float32)
    scaled = jnp.concatenate([value_rows[..., :HEAD_DIM] * key_scaling, value_rows[..., HEAD_DIM:]], axis=3)
    return scaled.astype(jnp.bfloat16)


def steps_of(own_key, extent, cuts, least, high):
    def one(axis_at, parts):
        steps = jax.random.uniform(jax.random.fold_in(jax.random.fold_in(own_key, 6), axis_at), (parts,), jnp.float32, least / len(cuts), high / len(cuts))
        return jnp.repeat(jnp.exp(steps), extent[axis_at] // parts).reshape((-1,) + (1,) * (len(extent) - axis_at - 1))

    gain = one(*cuts[0])
    for cut in cuts[1:]:
        gain = gain * one(*cut)
    return gain


def split_up(amount, total, reach, skew):
    loads = [(1 << 20) // math.isqrt(standing ** skew) + 1 for standing in range(2, amount + 1)]
    spare, given = total - reach - (amount - 1), [1] * (amount - 1)
    while spare > 0:
        free = [i for i in range(amount - 1) if given[i] < reach]
        whole, left = sum([loads[i] for i in free]), spare
        for i in free:
            more = min(reach - given[i], max(1, left * loads[i] // whole), spare)
            given[i] = given[i] + more
            spare = spare - more
    return np.array([reach] + given)


def uneven(key, count, total, limit, slope):
    if count == 2:
        one = jax.random.randint(key, (), max(1, total - limit), min(limit, total - 1) + 1)
        return jnp.stack([one, total - one])
    lengths = jnp.asarray(split_up(count, total, limit, slope), jnp.int32)
    pairs = (count - 1) // 2
    source_of, taker = lengths[1:1 + 2 * pairs:2], lengths[2:2 + 2 * pairs:2]
    margin = jnp.minimum(source_of - 1, limit - taker)
    shifted = jax.random.randint(jax.random.fold_in(key, 1), (pairs,), 0, 1 << 20) % (margin + 1)
    lengths = lengths.at[1:1 + 2 * pairs:2].set(source_of - shifted).at[2:2 + 2 * pairs:2].set(taker + shifted)
    return lengths[jax.random.permutation(jax.random.fold_in(key, 2), count)]


def routed_block(rng, own, number, rows, count, top, limit, skew):
    ranking = jax.random.permutation(rng, count)
    crowded, usual = portions_of(count, rows * top, limit, skew, True), portions_of(count, rows * top, limit, skew, False)
    places = jnp.arange(count)

    def named(sizes, offset_by):
        used = int((sizes > 0).sum())
        fixed = max(1, used // 4)
        shifted = fixed + (places - fixed + offset_by * (used - fixed)) % max(1, count - fixed)
        return jnp.zeros((count,), jnp.int32).at[ranking[jnp.where(places < fixed, places, shifted)]].set(jnp.asarray(sizes, jnp.int32))

    sizes = jnp.where(number % 4 == 0, named(crowded, number // 4), named(usual, number - number // 4 - 1))
    mixed = jax.random.permutation(jax.random.fold_in(own, 3), count)
    source_of, taker = mixed[0:count // 2 * 2:2], mixed[1:count // 2 * 2:2]
    margin = jnp.minimum(sizes[source_of] - 1, limit - sizes[taker]) // 2
    margin = jnp.where((source_of == ranking[0]) | (taker == ranking[0]) | (sizes[taker] == 0), 0, jnp.maximum(margin, 0))
    shifted = jax.random.randint(jax.random.fold_in(own, 4), (count // 2,), 0, 1 << 20) % (margin + 1)
    sizes = sizes.at[source_of].add(-shifted).at[taker].add(shifted)
    items = jnp.searchsorted(jnp.cumsum(sizes), jnp.arange(rows * top), side="right").astype(jnp.int32)
    grid = items.reshape(top, rows).T
    grid = grid[jax.random.permutation(jax.random.fold_in(own, 1), rows)]
    offset_by = jax.random.randint(jax.random.fold_in(own, 2), (rows, 1), 0, top)
    return jnp.take_along_axis(grid, (jnp.arange(top)[None, :] + offset_by) % top, axis=1)


def portions_of(amount, total, bound, slope, full):
    portions = [(1 << 20) // math.isqrt(rank ** slope) + 1 for rank in range(1, amount + 1)]
    largest = bound if full else min(bound, max(-(-total // amount), total * portions[0] // sum(portions)))
    least = 1 if total - largest >= amount - 1 else 0
    given, surplus = [largest] + [least] * (amount - 1), total - largest - least * (amount - 1)
    while surplus > 0:
        movable = [i for i in range(1, amount) if given[i] < largest] or [i for i in range(1, amount) if given[i] < bound]
        whole, left = sum([portions[i] for i in movable]), surplus
        for i in movable:
            more = min(bound - given[i], max(1, left * portions[i] // whole), surplus)
            given[i] = given[i] + more
            surplus = surplus - more
    return np.array(given)


def scatter_about(own_key, extent, scale, reach, shards=(), kind=jnp.bfloat16):
    values = jax.random.normal(own_key, extent, jnp.float32) * scale
    if len(shards) > 0:
        values = steps_of(own_key, extent, shards, -0.22, 0.18) * values
    return jnp.clip(values, min=-reach, max=reach).astype(kind)


def setup_inputs(seed: int = 0) -> dict:
    splits = jax.random.split(jax.random.key(seed), 13)
    tokens = scatter_about(splits[0], (TOKENS, MODEL_DIM), 1.0, 6.0, ((0, 8), (1, 4)))
    new_counts = jax.vmap(lambda own: uneven(own, REQ_DEV, TOK_DEV, MOSTN, 2))(jax.random.split(splits[1], (REQUEST_TOTAL // REQ_DEV))).reshape((REQUEST_TOTAL // REQ_DEV, REQ_DEV)).astype(jnp.int32)
    kv_cache = draw_kv_cache(jax.random.fold_in(splits[12], 71), 0)
    norm_attn = jnp.clip(1.0 + 0.18 * jax.random.normal(splits[3], (MODEL_DIM,), jnp.float32), 0.1, 1.9)
    query_weight = scatter_about(splits[4], (MODEL_DIM, KEY_HEADS, QUERY_PER_KV * HEAD_DIM), MODEL_DIM ** -0.5, 0.15625, ((1, 4),))
    key_value_weight = scatter_about(splits[5], (MODEL_DIM, KEY_HEADS, 2 * HEAD_DIM), (MODEL_DIM // 9) ** -0.5, 0.4375, ((1, 4),))
    output_weight = scatter_about(splits[6], (KEY_HEADS, QUERY_PER_KV * HEAD_DIM, MODEL_DIM), (QUERY_HEADS * HEAD_DIM) ** -0.5, 0.15625, ((0, 4),))
    norm_moe = jnp.clip(1.0 + 0.18 * jax.random.normal(splits[7], (MODEL_DIM,), jnp.float32), 0.1, 1.9)
    routes_keys = jax.random.split(jax.random.fold_in(splits[8], 1), TOKENS // MT)
    routes_turns = jax.random.permutation(jax.random.fold_in(splits[8], 3), TOKENS // MT)
    routes = jax.vmap(lambda own, number: routed_block(jax.random.fold_in(splits[8], 2), own, number, MT, EXPERTS, TOPK, CAP, 2))(routes_keys, routes_turns).reshape((TOKENS, TOPK))
    route_gain = jnp.clip(jnp.exp(math.log(0.3) - 2.3025852 * jax.random.uniform(splits[9], (TOKENS, TOPK), jnp.float32) ** steps_of(splits[9], (TOKENS, TOPK), ((0, 32),), -0.2, 0.2)), 0.03, 0.3)
    w_gate_up = scatter_about(splits[10], (EXPERTS, MODEL_DIM, 2 * FF), MODEL_DIM ** -0.5, 0.15625, ((0, 8),))
    w_down = scatter_about(splits[11], (EXPERTS, FF, MODEL_DIM), FF ** -0.5, 0.25, ((0, 8),))
    return dict(tokens=tokens, new_counts=new_counts, kv_cache=kv_cache, norm_attn=norm_attn, query_weight=query_weight, key_value_weight=key_value_weight, output_weight=output_weight, norm_moe=norm_moe, routes=routes, route_gain=route_gain, w_gate_up=w_gate_up, w_down=w_down)


floor_score = -1e+30

def norm_rows(value_rows, gain_row):
    mean_square = lax.optimization_barrier(jnp.mean(value_rows * value_rows, axis=-1, keepdims=True))
    return value_rows * lax.rsqrt(mean_square + 1e-05) * gain_row

def rope_tables(position, head_size):
    half_size = head_size // 2
    inverse = jnp.exp(jnp.arange(half_size, dtype=jnp.float32) * (-2.0 * math.log(10000.0) / head_size))
    angles = position.astype(jnp.float32)[:, None] * inverse[None, :]
    angles = jnp.concatenate([angles, angles], axis=1)
    return (jnp.cos(angles), jnp.sin(angles))

def rotate(vectors, cos_part, sin_part):
    half_size = vectors.shape[-1] // 2
    turned = jnp.concatenate([-vectors[..., half_size:], vectors[..., :half_size]], axis=-1)
    return vectors * cos_part + turned * sin_part

def request_layout(counts, token_count, cache_ratio):
    counts = counts.astype(jnp.int32)
    end_rows = jnp.cumsum(counts).astype(jnp.int32)
    starts = (end_rows - counts).astype(jnp.int32)
    row_ids = jnp.arange(token_count, dtype=jnp.int32)
    segment = lax.optimization_barrier(jnp.sum((row_ids[:, None] >= end_rows[None, :]).astype(jnp.int32), axis=1)).astype(jnp.int32)
    member = (segment[:, None] == jnp.arange(counts.shape[0], dtype=jnp.int32)[None, :]).astype(jnp.int32)
    row_begin = lax.optimization_barrier(jnp.sum(member * starts[None, :], axis=1)).astype(jnp.int32)
    own_count = lax.optimization_barrier(jnp.sum(member * counts[None, :], axis=1)).astype(jnp.int32)
    position = (cache_ratio * own_count + row_ids - row_begin).astype(jnp.int32)
    return (starts, position)

def project(normed, query_weight, key_value_weight, position):
    token_count, model_width = normed.shape
    kv_heads = key_value_weight.shape[1]
    head_size = key_value_weight.shape[2] // 2
    group_size = query_weight.shape[2] // head_size
    query = jnp.dot(normed, query_weight.reshape(model_width, -1), preferred_element_type=jnp.float32)
    query = query.reshape(token_count, kv_heads, group_size, head_size)
    keyval = jnp.dot(normed, key_value_weight.reshape(model_width, -1), preferred_element_type=jnp.float32)
    keyval = keyval.reshape(token_count, kv_heads, 2 * head_size)
    cos_part, sin_part = rope_tables(position, head_size)
    query = rotate(query, cos_part[:, None, None, :], sin_part[:, None, None, :]).astype(jnp.bfloat16)
    new_key = rotate(keyval[..., :head_size], cos_part[:, None, :], sin_part[:, None, :]).astype(jnp.bfloat16)
    new_value = keyval[..., head_size:].astype(jnp.bfloat16)
    return (query, new_key, new_value)

def round_half(value_rows):
    return lax.optimization_barrier(value_rows.astype(jnp.bfloat16)).astype(jnp.float32)

def attend_group(normed, counts, cache, query_weight, key_value_weight):
    token_count = normed.shape[0]
    counts = counts.astype(jnp.int32)
    starts, position = request_layout(counts, token_count, RATIO)
    query, new_key, new_value = project(normed, query_weight, key_value_weight, position)
    head_size = new_key.shape[-1]
    window = token_count // 2
    score_scale = 1.0 / math.sqrt(head_size)
    cache_len = cache.shape[2]

    def one_request(which, result):
        row_begin = starts[which]
        count_here = counts[which]
        cached = RATIO * count_here
        win_start = jnp.minimum(row_begin, token_count - window).astype(jnp.int32)
        row_ids = win_start + jnp.arange(window, dtype=jnp.int32)
        inside = (row_ids >= row_begin) & (row_ids < row_begin + count_here)
        q_win = lax.dynamic_slice_in_dim(query, win_start, window, 0).astype(jnp.float32)
        k_win = lax.dynamic_slice_in_dim(new_key, win_start, window, 0).astype(jnp.float32)
        v_win = lax.dynamic_slice_in_dim(new_value, win_start, window, 0).astype(jnp.float32)
        p_win = lax.dynamic_slice_in_dim(position, win_start, window, 0)
        past = lax.dynamic_index_in_dim(cache, which, 0, keepdims=False).astype(jnp.float32)
        old_ok = (jnp.arange(cache_len, dtype=jnp.int32) < cached)[None, None, None, :]
        new_ok = (inside[None, :] & (p_win[None, :] <= p_win[:, None]))[None, None, :, :]
        old_score = jnp.einsum('qhgd,hkd->hgqk', q_win, past[..., :head_size]) * score_scale
        new_score = jnp.einsum('qhgd,khd->hgqk', q_win, k_win) * score_scale
        old_score = jnp.where(old_ok, old_score, floor_score)
        new_score = jnp.where(new_ok, new_score, floor_score)
        highest = jnp.maximum(lax.optimization_barrier(jnp.max(old_score, axis=-1)), lax.optimization_barrier(jnp.max(new_score, axis=-1)))[..., None]
        old_exp = jnp.where(old_ok, jnp.exp(old_score - highest), 0.0)
        new_exp = jnp.where(new_ok, jnp.exp(new_score - highest), 0.0)
        denominator = lax.optimization_barrier(jnp.sum(old_exp, axis=-1)) + lax.optimization_barrier(jnp.sum(new_exp, axis=-1))
        numerator = jnp.einsum('hgqk,hkd->hgqd', round_half(old_exp), past[..., head_size:])
        numerator = numerator + jnp.einsum('hgqk,khd->hgqd', round_half(new_exp), v_win)
        attended = jnp.transpose(numerator / denominator[..., None], (2, 0, 1, 3))
        current = lax.dynamic_slice_in_dim(result, win_start, window, 0)
        update = jnp.where(inside[:, None, None, None], attended, current)
        return lax.dynamic_update_slice_in_dim(result, update, win_start, 0)
    initial = jnp.zeros(query.shape, jnp.float32)
    result = lax.fori_loop(0, counts.shape[0], one_request, initial)
    return result.astype(jnp.bfloat16)

def reference(tokens, new_counts, kv_cache, norm_attn, query_weight, key_value_weight, output_weight, norm_moe, routes, route_gain, w_gate_up, w_down):
    model_width = tokens.shape[1]
    groups = new_counts.shape[0]
    tok_groups = tokens.reshape(groups, TOK_DEV, model_width)
    cache_groups = kv_cache.reshape((groups, REQ_DEV) + kv_cache.shape[1:])
    out_blocks = output_weight.reshape(N_HEAD, -1, model_width).astype(jnp.float32)

    def group_step(inputs):
        tok_part, count_part, cache_part = inputs
        normed = norm_rows(tok_part.astype(jnp.float32), norm_attn).astype(jnp.bfloat16)
        attended = attend_group(normed, count_part, cache_part, query_weight, key_value_weight)
        flat_out = attended.reshape(TOK_DEV, N_HEAD, -1).astype(jnp.float32)
        partials = jnp.einsum('tjc,jcd->jtd', flat_out, out_blocks).astype(jnp.bfloat16)
        return tok_part.astype(jnp.float32) + lax.optimization_barrier(jnp.sum(partials.astype(jnp.float32), axis=0))
    resid = lax.map(group_step, (tok_groups, new_counts, cache_groups)).reshape(-1, model_width)
    moe_in = norm_rows(resid, norm_moe).astype(jnp.bfloat16)
    token_total = moe_in.shape[0]
    per_block = TOK_DEV // N_HEAD
    capacity = per_block // 2
    block_total = token_total // per_block
    route_blocks = routes.reshape(block_total, per_block * TOPK).astype(jnp.int32)
    expert_ids = jnp.arange(EXPERTS, dtype=jnp.int32)

    def slot_of(route_row):
        onehot = (route_row[:, None] == expert_ids[None, :]).astype(jnp.int32)
        before = (jnp.cumsum(onehot, axis=0) - onehot).astype(jnp.int32)
        rank_in = lax.optimization_barrier(jnp.sum(before * onehot, axis=1)).astype(jnp.int32)
        return (route_row * capacity + rank_in).astype(jnp.int32)
    slot_ids = jax.vmap(slot_of)(route_blocks)
    owners = jnp.arange(per_block * TOPK, dtype=jnp.int32) // TOPK

    def table_of(slot_row):
        return jnp.full((EXPERTS * capacity,), per_block, jnp.int32).at[slot_row].set(owners)
    tables = jax.vmap(table_of)(slot_ids)
    block_base = (jnp.arange(block_total, dtype=jnp.int32) * per_block)[:, None]
    token_slot = slot_ids.reshape(token_total, TOPK)
    token_block = jnp.arange(token_total, dtype=jnp.int32) // per_block
    ff_width = w_down.shape[1]

    def expert_step(running, expert):
        fill_ids = lax.dynamic_slice_in_dim(tables, expert * capacity, capacity, 1)
        present = (fill_ids < per_block).reshape(-1)
        source = (block_base + jnp.minimum(fill_ids, per_block - 1)).reshape(-1).astype(jnp.int32)
        picked = jnp.where(present[:, None], moe_in[source], jnp.zeros((), moe_in.dtype))
        gate_up = jnp.dot(picked, w_gate_up[expert], preferred_element_type=jnp.float32)
        hidden = (jax.nn.silu(gate_up[:, :ff_width]) * gate_up[:, ff_width:]).astype(jnp.bfloat16)
        produced = jnp.dot(hidden, w_down[expert], preferred_element_type=jnp.float32).astype(jnp.bfloat16)
        chosen = routes == expert
        rank_in = lax.optimization_barrier(jnp.sum(jnp.where(chosen, token_slot - expert * capacity, 0), axis=1)).astype(jnp.int32)
        weight = lax.optimization_barrier(jnp.sum(jnp.where(chosen, route_gain, 0.0), axis=1))
        gathered = produced[(token_block * capacity + rank_in).astype(jnp.int32)].astype(jnp.float32)
        return (running + weight[:, None] * gathered, None)
    moe_sum, _ = lax.scan(expert_step, jnp.zeros(resid.shape, jnp.float32), expert_ids)
    return (resid + moe_sum).astype(jnp.bfloat16)
```

```python
import functools
import math

import jax
import jax.numpy as jnp
from jax import lax
from jax.experimental import pallas as pl
from jax.experimental.pallas import tpu as pltpu
from jax.sharding import PartitionSpec as P

EXPERTS = 32
TOPK = 8
RATIO = 15
ROW_TILE = 176
KEY_TILE = 768
PART_TILE = 256
LOW = -1e30
MESH = pl.DeviceIdType.MESH
VMEM_BYTES = 56 * 1024 * 1024


def norm_rows(value_rows, gain_row):
    mean_square = jnp.mean(value_rows * value_rows, axis=-1, keepdims=True)
    return value_rows * lax.rsqrt(mean_square + 1e-05) * gain_row


def rope_tables(position, head_size):
    half_size = head_size // 2
    inverse = jnp.exp(
        jnp.arange(half_size, dtype=jnp.float32) * (-2.0 * math.log(10000.0) / head_size)
    )
    angles = position.astype(jnp.float32)[:, None] * inverse[None, :]
    angles = jnp.concatenate([angles, angles], axis=1)
    return (jnp.cos(angles), jnp.sin(angles))


def rotate(vectors, cos_part, sin_part):
    half_size = vectors.shape[-1] // 2
    turned = jnp.concatenate([-vectors[..., half_size:], vectors[..., :half_size]], axis=-1)
    return vectors * cos_part + turned * sin_part


def request_layout(counts, token_count, cache_ratio):
    end_rows = jnp.cumsum(counts)
    starts = end_rows - counts
    row_ids = jnp.arange(token_count, dtype=jnp.int32)
    segment = jnp.sum((row_ids[:, None] >= end_rows[None, :]).astype(jnp.int32), axis=1)
    member = (segment[:, None] == jnp.arange(counts.shape[0], dtype=jnp.int32)[None, :]).astype(
        jnp.int32
    )
    row_begin = jnp.sum(member * starts[None, :], axis=1)
    own_count = jnp.sum(member * counts[None, :], axis=1)
    position = cache_ratio * own_count + row_ids - row_begin
    return (starts, position)


def greet(axis, length, fast, line_at, fast_at):
    barrier = pltpu.get_barrier_semaphore()

    def to(index):
        pl.semaphore_signal(barrier, inc=1, device_id={axis: index}, device_id_type=MESH)

    for step in range(1, fast):
        to(line_at * fast + lax.rem(fast_at + step, fast))

    @pl.when(line_at > 0)
    def _():
        to((line_at - 1) * fast + fast_at)

    @pl.when(line_at < length - 1)
    def _():
        to((line_at + 1) * fast + fast_at)

    peers = fast - 1
    if length > 1:
        for away in (line_at, length - 1 - line_at):
            peers = peers + lax.div(away + length - 2, length - 1)
    pl.semaphore_wait(barrier, peers)


def gather_kernel(
    axis, length, fast, by_columns, x_ref, out_ref, own_sem, up_s, up_r, down_s, down_r, fast_s, fast_r
):
    me = lax.axis_index(axis)
    line_at, fast_at = me // fast, lax.rem(me, fast)
    width = x_ref.shape[1]

    def place(index):
        if by_columns:
            return out_ref.at[:, pl.ds(pl.multiple_of(index * width, 128), width)]
        return out_ref.at[index]

    greet(axis, length, fast, line_at, fast_at)

    own = pltpu.make_async_copy(x_ref, place(me), own_sem)
    own.start()

    def line_copy(step, sign):
        source = line_at - sign * step
        send, recv = (up_s, up_r) if sign > 0 else (down_s, down_r)
        block = place(source * fast + fast_at)
        return pltpu.make_async_remote_copy(
            src_ref=x_ref if step == 0 else block,
            dst_ref=block,
            send_sem=send.at[step],
            recv_sem=recv.at[step],
            device_id={axis: (line_at + sign) * fast + fast_at},
            device_id_type=MESH,
        )

    def line_arrival(step, sign):
        source = line_at - sign * step
        recv = up_r if sign > 0 else down_r
        block = place(source * fast + fast_at)
        pltpu.make_async_copy(block, block, recv.at[step - 1]).wait()

    def fast_copy(turn, step, sign):
        source = line_at - sign * step
        slot = step if sign > 0 else length - 1 + step
        block = place(source * fast + fast_at)
        return pltpu.make_async_remote_copy(
            src_ref=x_ref if step == 0 else block,
            dst_ref=block,
            send_sem=fast_s.at[turn - 1, slot],
            recv_sem=fast_r.at[turn - 1, slot],
            device_id={axis: line_at * fast + lax.rem(fast_at + turn, fast)},
            device_id_type=MESH,
        )

    def fast_arrival(turn, step, sign):
        source = line_at - sign * step
        slot = step if sign > 0 else length - 1 + step
        block = place(source * fast + lax.rem(fast_at - turn + fast, fast))
        pltpu.make_async_copy(block, block, fast_r.at[turn - 1, slot]).wait()

    def has_next(sign):
        return line_at < length - 1 if sign > 0 else line_at > 0

    def has_source(step, sign):
        return line_at >= step if sign > 0 else line_at + step < length

    for sign in (1, -1):

        @pl.when(has_next(sign))
        def _():
            line_copy(0, sign).start()

    for turn in range(1, fast):
        fast_copy(turn, 0, 1).start()

    for step in range(1, length):
        for sign in (1, -1):

            @pl.when(has_source(step, sign))
            def _():
                line_arrival(step, sign)

                @pl.when(has_next(sign))
                def _():
                    line_copy(step, sign).start()

                for turn in range(1, fast):
                    fast_copy(turn, step, sign).start()

    for turn in range(1, fast):
        fast_arrival(turn, 0, 1)
        fast_copy(turn, 0, 1).wait_send()
    for sign in (1, -1):

        @pl.when(has_next(sign))
        def _():
            line_copy(0, sign).wait_send()

        for step in range(1, length):

            @pl.when(has_source(step, sign))
            def _():
                @pl.when(has_next(sign))
                def _():
                    line_copy(step, sign).wait_send()

                for turn in range(1, fast):
                    fast_arrival(turn, step, sign)
                    fast_copy(turn, step, sign).wait_send()

    own.wait()


def gather_over(value, axis, length, ident, by_columns):
    count = lax.axis_size(axis)
    fast = count // length
    rows, width = value.shape
    shape = (rows, count * width) if by_columns else (count, rows, width)
    dma = pltpu.SemaphoreType.DMA
    return pl.pallas_call(
        functools.partial(gather_kernel, axis, length, fast, by_columns),
        out_shape=jax.ShapeDtypeStruct(shape, value.dtype),
        in_specs=[pl.BlockSpec(memory_space=pl.ANY)],
        out_specs=pl.BlockSpec(memory_space=pl.ANY),
        scratch_shapes=[
            dma,
            dma((length,)),
            dma((length,)),
            dma((length,)),
            dma((length,)),
            dma((max(fast - 1, 1), 2 * length - 1)),
            dma((max(fast - 1, 1), 2 * length - 1)),
        ],
        compiler_params=pltpu.CompilerParams(
            collective_id=ident, has_side_effects=True, vmem_limit_bytes=VMEM_BYTES
        ),
        name="gather_" + axis,
    )(value)


def scatter_kernel(
    axis, length, fast, parts_ref, out_ref, near, up_in, down_in, up_out, down_out,
    near_s, near_r, up_s, up_r, down_s, down_r,
):
    me = lax.axis_index(axis)
    line_at, fast_at = me // fast, lax.rem(me, fast)
    rows = out_ref.shape[0]
    chunk = 32
    greet(axis, length, fast, line_at, fast_at)

    def slot_of(step, sign):
        return step if sign > 0 else length - 1 + step

    def there(step, sign):
        return line_at + step < length if sign > 0 else line_at >= step

    def near_copy(turn, step, sign):
        target = line_at + sign * step
        other = lax.rem(fast_at + turn, fast)
        return pltpu.make_async_remote_copy(
            src_ref=parts_ref.at[target * fast + other],
            dst_ref=near.at[turn - 1, target],
            send_sem=near_s.at[turn - 1, slot_of(step, sign)],
            recv_sem=near_r.at[turn - 1, slot_of(step, sign)],
            device_id={axis: line_at * fast + other},
            device_id_type=MESH,
        )

    def line_copy(step, sign):
        outgoing, incoming = (up_out, up_in) if sign > 0 else (down_out, down_in)
        send, recv = (up_s, up_r) if sign > 0 else (down_s, down_r)
        return pltpu.make_async_remote_copy(
            src_ref=outgoing.at[step - 1],
            dst_ref=incoming.at[step - 1],
            send_sem=send.at[step - 1],
            recv_sem=recv.at[step - 1],
            device_id={axis: (line_at + sign) * fast + fast_at},
            device_id_type=MESH,
        )

    def start_near(step):
        for sign in (1, -1) if step > 0 else (1,):

            @pl.when(there(step, sign))
            def _():
                for turn in range(1, fast):
                    near_copy(turn, step, sign).start()

    def add_up(target, extra, store):
        @pl.loop(0, rows // chunk)
        def _(piece):
            span = pl.ds(pl.multiple_of(piece * chunk, chunk), chunk)
            total = parts_ref[target * fast + fast_at, span, :].astype(jnp.float32)
            for turn in range(1, fast):
                total = total + near[turn - 1, target, span, :].astype(jnp.float32)
            for incoming, slot in extra:
                total = total + incoming[slot, span, :].astype(jnp.float32)
            store(span, total)

    def near_arrival(step, sign):
        for turn in range(1, fast):
            near_copy(turn, step, sign).wait_recv()

    start_near(length - 1)
    if length > 1:
        start_near(length - 2)
    for step in range(length - 1, 0, -1):
        for sign in (1, -1):
            outgoing, incoming = (up_out, up_in) if sign > 0 else (down_out, down_in)
            has_before = line_at > 0 if sign > 0 else line_at < length - 1

            def store(span, total):
                outgoing[step - 1, span, :] = total.astype(outgoing.dtype)

            @pl.when(there(step, sign))
            def _():
                near_arrival(step, sign)
                target = line_at + sign * step
                if step < length - 1:

                    @pl.when(has_before)
                    def _():
                        line_copy(step + 1, sign).wait_recv()
                        add_up(target, [(incoming, step)], store)

                    @pl.when(jnp.logical_not(has_before))
                    def _():
                        add_up(target, [], store)
                else:
                    add_up(target, [], store)
                line_copy(step, sign).start()

        if step >= 2:
            start_near(step - 2)

    near_arrival(0, 1)

    def store_out(span, total):
        out_ref[span, :] = total

    def add_out(span, total):
        out_ref[span, :] = out_ref[span, :] + total

    add_up(line_at, [], store_out)
    if length > 1:
        for sign in (1, -1):
            incoming = up_in if sign > 0 else down_in
            has_before = line_at > 0 if sign > 0 else line_at < length - 1

            @pl.when(has_before)
            def _():
                line_copy(1, sign).wait_recv()

                @pl.loop(0, rows // chunk)
                def _(piece):
                    span = pl.ds(pl.multiple_of(piece * chunk, chunk), chunk)
                    add_out(span, incoming[0, span, :].astype(jnp.float32))

    for step in range(length - 1, -1, -1):
        for sign in (1, -1) if step > 0 else (1,):

            @pl.when(there(step, sign))
            def _():
                for turn in range(1, fast):
                    near_copy(turn, step, sign).wait_send()
                if step > 0:
                    line_copy(step, sign).wait_send()


def scatter_over(parts, axis, length, ident):
    count, rows, width = parts.shape
    fast = count // length
    dma = pltpu.SemaphoreType.DMA
    hops = max(length - 1, 1)
    turns = max(fast - 1, 1)
    line_shape = pltpu.VMEM((hops, rows, width), parts.dtype)
    return pl.pallas_call(
        functools.partial(scatter_kernel, axis, length, fast),
        out_shape=jax.ShapeDtypeStruct((rows, width), jnp.float32),
        in_specs=[pl.BlockSpec(memory_space=pltpu.VMEM)],
        out_specs=pl.BlockSpec(memory_space=pltpu.VMEM),
        scratch_shapes=[
            pltpu.VMEM((turns, length, rows, width), parts.dtype),
            line_shape,
            line_shape,
            line_shape,
            line_shape,
            dma((turns, 2 * length - 1)),
            dma((turns, 2 * length - 1)),
            dma((hops,)),
            dma((hops,)),
            dma((hops,)),
            dma((hops,)),
        ],
        compiler_params=pltpu.CompilerParams(
            collective_id=ident, has_side_effects=True, vmem_limit_bytes=VMEM_BYTES
        ),
        name="scatter_" + axis,
    )(parts)


def attend_kernel(starts_ref, counts_ref, q_ref, key_ref, value_ref, past_ref, out_ref, top_ref, sum_ref):
    which = pl.program_id(1)
    begin = starts_ref[which]
    count = counts_ref[which]
    cached = RATIO * count
    base = (begin // 16) * 16
    heads = q_ref.shape[1]
    size = out_ref.shape[3]
    tiles = (begin + count - base + ROW_TILE - 1) // ROW_TILE
    whole = cached // KEY_TILE
    rest = (cached - whole * KEY_TILE + PART_TILE - 1) // PART_TILE

    def absorb(head, query, keys, values, ok):
        scores = lax.dot_general(
            query, keys, (((1,), (1,)), ((), ())), preferred_element_type=jnp.float32
        )
        if ok is not None:
            scores = jnp.where(ok, scores, LOW)
        old_top = top_ref[head]
        new_top = jnp.maximum(old_top, jnp.max(scores, axis=1, keepdims=True))
        top_ref[head] = new_top
        weights = jnp.exp2((scores - new_top[:, :1]).astype(jnp.bfloat16))
        sum_ref[head] = sum_ref[head] * jnp.exp2(old_top - new_top) + jnp.dot(
            weights, values, preferred_element_type=jnp.float32
        )

    @pl.loop(0, tiles)
    def _(tile):
        row = pl.multiple_of(base + tile * ROW_TILE, 16)
        span = pl.ds(row, ROW_TILE)
        for head in range(heads):
            top_ref[head] = jnp.full(top_ref.shape[1:], LOW, jnp.float32)
            sum_ref[head] = jnp.zeros(sum_ref.shape[1:], jnp.float32)

        new_blocks = (row + ROW_TILE - base + PART_TILE - 1) // PART_TILE

        @pl.loop(0, new_blocks)
        def _(block):
            first = pl.multiple_of(base + block * PART_TILE, 16)
            keys = key_ref[0, pl.ds(first, PART_TILE), :]
            values = value_ref[0, pl.ds(first, PART_TILE), :]
            key_rows = first + lax.broadcasted_iota(jnp.int32, (ROW_TILE, PART_TILE), 1)
            own_rows = row + lax.broadcasted_iota(jnp.int32, (ROW_TILE, PART_TILE), 0)
            ok = (key_rows >= begin) & (key_rows <= own_rows)
            for head in range(heads):
                absorb(head, q_ref[0, head, span, :], keys, values, ok)

        def cache_rows(first, amount):
            keys = past_ref[0, 0, pl.ds(first, amount), :]
            lanes = lax.broadcasted_iota(jnp.int32, keys.shape, 1)
            return keys, jnp.where(lanes < size, jnp.ones_like(keys), keys)

        @pl.loop(0, whole)
        def _(block):
            keys, values = cache_rows(pl.multiple_of(block * KEY_TILE, KEY_TILE), KEY_TILE)
            for head in range(heads):
                absorb(head, q_ref[0, head, span, :], keys, values, None)

        @pl.loop(0, rest)
        def _(block):
            first = pl.multiple_of(whole * KEY_TILE + block * PART_TILE, PART_TILE)
            keys, values = cache_rows(first, PART_TILE)
            slots = first + lax.broadcasted_iota(jnp.int32, (ROW_TILE, PART_TILE), 1)
            for head in range(heads):
                absorb(head, q_ref[0, head, span, :], keys, values, slots < cached)

        rows = row + lax.broadcasted_iota(jnp.int32, (ROW_TILE, size), 0)
        inside = (rows >= begin) & (rows < begin + count)
        for head in range(heads):
            total = sum_ref[head]
            attended = (total[:, size:] / total[:, :size]).astype(out_ref.dtype)
            out_ref[0, head, span, :] = jnp.where(inside, attended, out_ref[0, head, span, :])


def attend(starts, counts, query, keys, values, kv_cache):
    kv_heads, heads, rows, lanes = query.shape
    requests, _, slots, _ = kv_cache.shape
    size = lanes // 2
    return pl.pallas_call(
        attend_kernel,
        out_shape=jax.ShapeDtypeStruct((kv_heads, heads, rows, size), jnp.bfloat16),
        grid_spec=pltpu.PrefetchScalarGridSpec(
            num_scalar_prefetch=2,
            grid=(kv_heads, requests),
            in_specs=[
                pl.BlockSpec((1, heads, rows, lanes), lambda h, r, s, c: (h, 0, 0, 0)),
                pl.BlockSpec((1, rows, lanes), lambda h, r, s, c: (h, 0, 0)),
                pl.BlockSpec((1, rows, lanes), lambda h, r, s, c: (h, 0, 0)),
                pl.BlockSpec((1, 1, slots, lanes), lambda h, r, s, c: (r, h, 0, 0)),
            ],
            out_specs=pl.BlockSpec((1, heads, rows, size), lambda h, r, s, c: (h, 0, 0, 0)),
            scratch_shapes=[
                pltpu.VMEM((heads, ROW_TILE, lanes), jnp.float32),
                pltpu.VMEM((heads, ROW_TILE, lanes), jnp.float32),
            ],
        ),
        compiler_params=pltpu.CompilerParams(vmem_limit_bytes=VMEM_BYTES),
        name="attend",
    )(starts, counts, query, keys, values, kv_cache)


def expert_kernel(
    capacity, rank_row_ref, rank_col_ref, gain_col_ref, x_ref, up_hbm, down_hbm, out_ref,
    up_ref, down_ref, total_ref, sems,
):
    group, per_block, _ = x_ref.shape
    experts = up_ref.shape[0]
    ff_width = down_ref.shape[1]
    first = pl.program_id(0) == 0

    def fetch(expert):
        return (
            pltpu.make_async_copy(up_hbm.at[expert], up_ref.at[expert], sems.at[0, expert]),
            pltpu.make_async_copy(down_hbm.at[expert], down_ref.at[expert], sems.at[1, expert]),
        )

    @pl.when(first)
    def _():
        for expert in range(experts):
            for copy in fetch(expert):
                copy.start()

    for expert in range(experts):

        @pl.when(first)
        def _():
            for copy in fetch(expert):
                copy.wait()

        slot_rows = lax.broadcasted_iota(jnp.int32, (capacity, per_block), 0)
        slot_cols = lax.broadcasted_iota(jnp.int32, (per_block, capacity), 1)
        picked = []
        for item in range(group):
            ranks = rank_row_ref[item, expert : expert + 1, :]
            choose = (slot_rows == ranks).astype(jnp.float32).astype(jnp.bfloat16)
            picked.append(
                jnp.dot(choose, x_ref[item], preferred_element_type=jnp.float32).astype(jnp.bfloat16)
            )
        picked = jnp.concatenate(picked, axis=0)
        both = jnp.dot(picked, up_ref[expert], preferred_element_type=jnp.float32)
        gate = both[:, :ff_width]
        hidden = (gate / (1.0 + jnp.exp(-gate)) * both[:, ff_width:]).astype(jnp.bfloat16)
        made = jnp.dot(hidden, down_ref[expert], preferred_element_type=jnp.float32).astype(
            jnp.bfloat16
        )
        for item in range(group):
            ranks = rank_col_ref[item, :, expert : expert + 1]
            gains = gain_col_ref[item, :, expert : expert + 1]
            blend = jnp.where(slot_cols == ranks, gains, 0.0).astype(jnp.bfloat16)
            part = jnp.dot(
                blend,
                made[item * capacity : (item + 1) * capacity],
                preferred_element_type=jnp.float32,
            )
            if expert > 0:
                part = total_ref[item] + part
            if expert < experts - 1:
                total_ref[item] = part
            else:
                out_ref[item] = part.astype(out_ref.dtype)


def run_experts(rank_col, gain_col, rows, w_gate_up, w_down, capacity):
    sources, per_block, width = rows.shape
    experts = w_down.shape[0]
    group = min(sources, max(1, 256 // capacity))
    rank_row = jnp.swapaxes(rank_col, 1, 2)
    return pl.pallas_call(
        functools.partial(expert_kernel, capacity),
        out_shape=jax.ShapeDtypeStruct((sources, per_block, width), jnp.bfloat16),
        grid=(sources // group,),
        in_specs=[
            pl.BlockSpec((group, experts, per_block), lambda s: (s, 0, 0)),
            pl.BlockSpec((group, per_block, experts), lambda s: (s, 0, 0)),
            pl.BlockSpec((group, per_block, experts), lambda s: (s, 0, 0)),
            pl.BlockSpec((group, per_block, width), lambda s: (s, 0, 0)),
            pl.BlockSpec(memory_space=pl.ANY),
            pl.BlockSpec(memory_space=pl.ANY),
        ],
        out_specs=pl.BlockSpec((group, per_block, width), lambda s: (s, 0, 0)),
        scratch_shapes=[
            pltpu.VMEM(w_gate_up.shape, w_gate_up.dtype),
            pltpu.VMEM(w_down.shape, w_down.dtype),
            pltpu.VMEM((group, per_block, width), jnp.float32),
            pltpu.SemaphoreType.DMA((2, experts)),
        ],
        compiler_params=pltpu.CompilerParams(vmem_limit_bytes=VMEM_BYTES),
        name="experts",
    )(rank_row, rank_col, gain_col, rows, w_gate_up, w_down)


def local(
    req_line,
    head_line,
    tokens,
    new_counts,
    kv_cache,
    norm_attn,
    query_weight,
    key_value_weight,
    output_weight,
    norm_moe,
    routes,
    route_gain,
    w_gate_up,
    w_down,
):
    per_block = routes.shape[0]
    capacity = per_block // 2
    per_req = w_down.shape[0]

    table = jnp.concatenate([routes.astype(jnp.float32), route_gain], axis=1)
    table = lax.all_gather(table, "req", axis=0)
    all_routes = table[..., :TOPK]
    own_ids = lax.axis_index("req") * per_req + jnp.arange(per_req, dtype=jnp.int32)
    named = all_routes[:, :, :, None] == own_ids.astype(jnp.float32)[None, None, None, :]
    chosen = jnp.any(named, axis=2)
    gain_col = jnp.sum(jnp.where(named, table[..., TOPK:, None], 0.0), axis=2)
    earlier = jnp.tril(jnp.ones((per_block, per_block), jnp.bfloat16), -1)
    rank_col = jnp.einsum(
        "tu,sun->stn", earlier, chosen.astype(jnp.bfloat16), preferred_element_type=jnp.float32
    )
    rank_col = jnp.where(chosen, rank_col.astype(jnp.int32), -1)

    if tokens.shape[1] % 128 == 0:
        whole = gather_over(tokens, "head", head_line, 0, True)
    else:
        narrow = tokens.shape[1]
        spread = jnp.pad(tokens, ((0, 0), (0, -narrow % 128)))
        whole = gather_over(spread, "head", head_line, 0, False)[..., :narrow]
        whole = jnp.swapaxes(whole, 0, 1).reshape(tokens.shape[0], -1)
    token_count, model_width = whole.shape
    normed = norm_rows(whole.astype(jnp.float32), norm_attn).astype(jnp.bfloat16)
    counts = new_counts[0]
    starts, position = request_layout(counts, token_count, RATIO)
    kv_heads = key_value_weight.shape[1]
    size = key_value_weight.shape[2] // 2
    groups = query_weight.shape[2] // size
    cos_part, sin_part = rope_tables(position, size)
    query = jnp.dot(
        normed, query_weight.reshape(model_width, -1), preferred_element_type=jnp.float32
    ).reshape(token_count, kv_heads, groups, size)
    keyval = jnp.dot(
        normed, key_value_weight.reshape(model_width, -1), preferred_element_type=jnp.float32
    ).reshape(token_count, kv_heads, 2 * size)
    scale = math.log2(math.e) / math.sqrt(size)
    query = rotate(query, cos_part[:, None, None, :], sin_part[:, None, None, :]) * scale
    query = jnp.transpose(query.astype(jnp.bfloat16), (1, 2, 0, 3))
    new_key = rotate(keyval[..., :size], cos_part[:, None, :], sin_part[:, None, :])
    new_key = jnp.transpose(new_key.astype(jnp.bfloat16), (1, 0, 2))
    new_value = jnp.transpose(keyval[..., size:].astype(jnp.bfloat16), (1, 0, 2))
    spare = 512
    query = jnp.pad(query, ((0, 0), (0, 0), (0, spare), (0, size)))
    new_key = jnp.pad(new_key, ((0, 0), (0, spare), (0, size)))
    new_value = jnp.pad(
        jnp.concatenate([jnp.ones_like(new_value), new_value], axis=2), ((0, 0), (0, spare), (0, 0))
    )
    attended = attend(starts, counts, query, new_key, new_value, kv_cache)[:, :, :token_count]
    flat = jnp.transpose(attended, (2, 0, 1, 3)).reshape(token_count, -1)
    partial_value = jnp.dot(
        flat, output_weight.reshape(-1, model_width), preferred_element_type=jnp.float32
    ).astype(jnp.bfloat16)
    attn_rows = scatter_over(
        partial_value.reshape(-1, per_block, model_width), "head", head_line, 1
    )
    row_start = lax.axis_index("head") * per_block
    base_rows = lax.dynamic_slice_in_dim(whole, row_start, per_block, 0)
    resid = base_rows.astype(jnp.float32) + attn_rows
    moe_in = norm_rows(resid, norm_moe).astype(jnp.bfloat16)
    everyone = gather_over(moe_in, "req", req_line, 2, False)
    parts = run_experts(rank_col, gain_col, everyone, w_gate_up, w_down, capacity)
    moe_sum = scatter_over(parts, "req", req_line, 3)
    return (resid + moe_sum).astype(jnp.bfloat16)


def solution(mesh):
    in_specs = (
        P("req", "head"),
        P("req", None),
        P("req", "head", None, None),
        P(),
        P(None, "head", None),
        P(None, "head", None),
        P("head", None, None),
        P(),
        P(("req", "head"), None),
        P(("req", "head"), None),
        P("req", None, None),
        P("req", None, None),
    )
    out_specs = P(("req", "head"), None)
    head_line = max(mesh.shape["head"] // 2, 1)
    req_line = math.gcd(mesh.shape["req"], 4)
    body = functools.partial(local, req_line, head_line)
    return jax.shard_map(body, mesh=mesh, in_specs=in_specs, out_specs=out_specs, check_vma=False)
```
